256 devices in a mesh: row: 8 (over z_hi, x), col: 32 (over z_lo, y, core).
Axes of the slice: x: 4, y: 4, z: 8 (z_hi: 2, z_lo: 4; z = z_hi * 4 + z_lo), core: 2. Of those that a mesh axis runs over, the one named last changes fastest.
Arguments:
- pair: float32 [512, 512, 128], P('row', 'col'), may hold values from -6 to 6
- pair_mask: int32 [512, 512], P('row', 'col'), may hold values 0 or 1
- norm_gain: float32 [128], replicated, may hold values from 0.1 to 1.9
- left_weight: bfloat16 [128, 256], replicated, may hold values from -0.5 to 0.5
- right_weight: bfloat16 [128, 256], replicated, may hold values from -0.5 to 0.5
- gate_weight: bfloat16 [128, 128], replicated, may hold values from -0.5 to 0.5
- out_gain: float32 [128], replicated, may hold values from 0.1 to 1.9
- out_weight: bfloat16 [128, 128], replicated, may hold values from -0.5 to 0.5
Outputs:
- update: bfloat16 [512, 512, 128], P('row', 'col')
The draws below stay inside these ranges and needn't reach their ends.
All inputs are finite; a program needn't handle non-finite values. No bound on the sum of `pair_mask` on one device may be relied on, other than what follows from the above.
Results may differ from the reference program's by a relative error of at most 0.0078.
Values may be sent and summed in bfloat16 or wider, within the bound.
A program may use at most 128 MiB of HBM per device.

```python
import jax
import jax.numpy as jnp
from jax import lax

C = 128
H = 128
N = 512


def set_ends(values, key, low, largest):
    dims = values.shape
    place = [jax.random.randint(jax.random.fold_in(key, axis), (), 0, dims[axis]) for axis in range(len(dims))]
    values = values.at[tuple(place)].set(low)
    longest = dims.index(max(dims))
    place[longest] = (place[longest] + 1) % dims[longest]
    return values.at[tuple(place)].set(largest)


def steps_of(stream_key, extent, pieces, least, high):
    def one(axis_at, shards_of):
        steps = jax.random.uniform(jax.random.fold_in(jax.random.fold_in(stream_key, 6), axis_at), (shards_of,), jnp.float32, least / len(pieces), high / len(pieces))
        return jnp.repeat(jnp.exp(steps), extent[axis_at] // shards_of).reshape((-1,) + (1,) * (len(extent) - axis_at - 1))

    loudness = one(*pieces[0])
    for cut in pieces[1:]:
        loudness = loudness * one(*cut)
    return loudness


def centred(key, shape, width, most, pieces=(), kind=jnp.bfloat16):
    level = steps_of(key, shape, pieces, -0.22, 0.18) if pieces else 1.0
    result = jax.random.normal(key, shape, jnp.float32) * width * level
    return jnp.minimum(jnp.maximum(result, -most), most).astype(kind)


def setup_inputs(seed: int = 0) -> dict:
    arg_keys = jax.random.split(jax.random.key(seed), 9)
    return {
        "pair": centred(arg_keys[0], (N, N, C), 1.0, 6.0, ((0, 8), (1, 32)), jnp.float32),
        "pair_mask": set_ends((jax.random.randint(arg_keys[1], (N, N), 0, 8) < 7).astype(jnp.int32), jax.random.fold_in(arg_keys[1], 1), 0, 1),
        "norm_gain": jnp.clip(1.0 + 0.18 * jax.random.normal(arg_keys[2], (C,), jnp.float32), 0.1, 1.9),
        "left_weight": centred(arg_keys[3], (C, 2 * H), C ** -0.5, 0.5),
        "right_weight": centred(arg_keys[4], (C, 2 * H), C ** -0.5, 0.5),
        "gate_weight": centred(arg_keys[5], (C, C), C ** -0.5, 0.5),
        "out_gain": jnp.clip(1.0 + 0.18 * jax.random.normal(arg_keys[6], (H,), jnp.float32), 0.1, 1.9),
        "out_weight": centred(arg_keys[7], (H, C), H ** -0.5, 0.5),
    }


def layer_norm(values, gain):
    mean = lax.optimization_barrier(jnp.mean(values, axis=-1, keepdims=True))
    centered = values - mean
    spread = lax.optimization_barrier(jnp.mean(centered * centered, axis=-1, keepdims=True))
    return centered * jax.lax.rsqrt(spread + 1e-05) * gain

def edges(normed, weight, mask_f):
    hidden = weight.shape[1] // 2
    proj = jnp.dot(normed, weight, preferred_element_type=jnp.float32)
    return (jax.nn.sigmoid(proj[..., :hidden]) * proj[..., hidden:] * mask_f).astype(jnp.bfloat16)

def reference(pair, pair_mask, norm_gain, left_weight, right_weight, gate_weight, out_gain, out_weight):
    normed = layer_norm(pair, norm_gain).astype(jnp.bfloat16)
    mask_f = pair_mask.astype(jnp.float32)[..., None]
    left = edges(normed, left_weight, mask_f)
    right = edges(normed, right_weight, mask_f)
    gate = jax.nn.sigmoid(jnp.dot(normed, gate_weight, preferred_element_type=jnp.float32))
    triangle = jnp.einsum('ikh,jkh->ijh', left.astype(jnp.float32), right.astype(jnp.float32))
    tri_normed = layer_norm(triangle, out_gain).astype(jnp.bfloat16)
    update = gate * jnp.dot(tri_normed, out_weight, preferred_element_type=jnp.float32)
    return update.astype(jnp.bfloat16)
```

```python
import jax
import jax.numpy as jnp
from jax import lax
from jax.experimental import pallas as pl
from jax.experimental.pallas import tpu as pltpu
from jax.sharding import PartitionSpec as P

F32 = jnp.float32
BF16 = jnp.bfloat16
EPS = 1e-05
CHIPS = 128


def rem(a, b):
    return lax.rem(a, jnp.int32(b))


def div(a, b):
    return lax.div(a, jnp.int32(b))


def kernel(
    pair_ref, mask_ref, norm_gain_ref, left_w_ref, right_w_ref, gate_w_ref, out_gain_ref, out_w_ref,
    out_ref,
    gate, edges, packed, send, recv, part, other, osend, orecv, flat, rows_out,
    send_sem, recv_sem, osend_sem, orecv_sem, xsend_sem, xrecv_sem,
):
    row = lax.axis_index("row")
    col = lax.axis_index("col")
    core = rem(col, 2)
    x = rem(row, 4)
    y = rem(div(col, 2), 4)
    z = div(row, 4) * 4 + div(col, 8)
    me = row * 16 + div(col, 2)

    def peer(step):
        pz = rem(z + rem(step, 8), 8)
        py = rem(y + rem(div(step, 8), 4), 4)
        px = rem(x + div(step, 32), 4)
        prow = div(pz, 4) * 4 + px
        pchip = rem(pz, 4) * 4 + py
        return prow * 16 + pchip, prow, pchip * 2 + core

    partner = {"col": col + 1 - 2 * core}

    barrier = pltpu.get_barrier_semaphore()

    def greet(step, carry):
        _, prow, pcol = peer(step)
        pl.semaphore_signal(barrier, inc=1, device_id=(prow, pcol), device_id_type=pl.DeviceIdType.MESH)
        return carry

    lax.fori_loop(1, CHIPS, greet, 0)
    pl.semaphore_signal(barrier, inc=1, device_id=partner, device_id_type=pl.DeviceIdType.MESH)

    gain = norm_gain_ref[...]
    for block in range(4):
        values = pair_ref[pl.ds(block * 16, 16)].reshape(256, 128)
        mean = jnp.mean(values, axis=-1, keepdims=True)
        centered = values - mean
        spread = jnp.mean(centered * centered, axis=-1, keepdims=True)
        normed = (centered * lax.rsqrt(spread + EPS) * gain).astype(BF16)
        here = pl.ds(block * 256, 256)
        for side, weight in ((0, left_w_ref), (1, right_w_ref)):
            proj = jnp.dot(normed, weight[...], preferred_element_type=F32)
            edges[side, here, :] = jax.nn.sigmoid(proj[:, :128]) * proj[:, 128:]
        gate[here, :] = jax.nn.sigmoid(jnp.dot(normed, gate_w_ref[...], preferred_element_type=F32))

    odd = rem(row, 2)
    for k in range(16):
        first = edges[odd, pl.ds(k, 64, stride=16), :]
        second = edges[1 - odd, pl.ds(k, 64, stride=16), :]
        packed[pl.ds(k, 128, stride=16), :] = jnp.concatenate([first, second], axis=0).T
    mask = mask_ref[...].astype(F32)
    mask = jnp.concatenate([mask, mask], axis=0).T
    send[...] = (packed[...].reshape(128, 16, 128) * mask[None]).astype(BF16)

    pl.semaphore_wait(barrier, CHIPS)

    own = pltpu.make_async_copy(send.at[me], recv.at[me], recv_sem)
    own.start()

    def scatter(step, carry):
        there, prow, pcol = peer(step)
        pltpu.make_async_remote_copy(
            src_ref=send.at[there], dst_ref=recv.at[me], send_sem=send_sem, recv_sem=recv_sem,
            device_id=(prow, pcol), device_id_type=pl.DeviceIdType.MESH,
        ).start()
        return carry

    lax.fori_loop(1, CHIPS, scatter, 0)
    pltpu.make_async_copy(recv, recv, recv_sem).wait()

    low = lax.broadcasted_iota(jnp.int32, (256, 128), 1) < 64
    lefts, rights = [], []
    for pair_at in range(4):
        even = recv[pl.ds(pair_at * 32, 16)].reshape(256, 128)
        uneven = recv[pl.ds(pair_at * 32 + 16, 16)].reshape(256, 128)
        lefts.append(jnp.where(low, even, uneven))
        rights.append(jnp.where(low, uneven, even))
    left = jnp.concatenate(lefts, axis=1)
    for pair_at in range(4):
        products = lax.dot_general(
            rights[pair_at], left, (((0,), (0,)), ((), ())), preferred_element_type=F32
        )
        for half in range(2):
            r = pair_at * 2 + 1 - half
            for q in range(4):
                at = half * 64 + q * 16
                part[q % 2, pl.ds((r * 2 + q // 2) * 16, 16), :] = products[at:at + 16]

    swap = pltpu.make_async_remote_copy(
        src_ref=part.at[1 - core], dst_ref=other, send_sem=xsend_sem, recv_sem=xrecv_sem,
        device_id=partner, device_id_type=pl.DeviceIdType.MESH,
    )
    swap.start()
    pltpu.make_async_copy(send.at[pl.ds(0, CHIPS - 1)], send.at[pl.ds(0, CHIPS - 1)], send_sem).wait()
    swap.wait_recv()

    low8 = lax.broadcasted_iota(jnp.int32, (256 // 2, 128), 1) < 64
    for pair_at in range(4):
        lanes = pl.ds(pair_at * 128, 128)
        total = (part[core, :, lanes] + other[:, lanes]).reshape(16, 2, 8, 128)
        top = total[:, 0].reshape(128, 128)
        bottom = total[:, 1].reshape(128, 128)
        even = jnp.where(low8, top, pltpu.roll(bottom, 64, 1))
        uneven = jnp.where(low8, pltpu.roll(top, 64, 1), bottom)
        osend[pl.ds(pair_at * 32, 16)] = even.reshape(16, 8, 128).astype(BF16)
        osend[pl.ds(pair_at * 32 + 16, 16)] = uneven.reshape(16, 8, 128).astype(BF16)

    own_back = pltpu.make_async_copy(osend.at[me], orecv.at[me], orecv_sem)
    own_back.start()

    def give_back(step, carry):
        there, prow, pcol = peer(step)
        pltpu.make_async_remote_copy(
            src_ref=osend.at[there], dst_ref=orecv.at[me], send_sem=osend_sem, recv_sem=orecv_sem,
            device_id=(prow, pcol), device_id_type=pl.DeviceIdType.MESH,
        ).start()
        return carry

    lax.fori_loop(1, CHIPS, give_back, 0)
    swap.wait_send()
    pltpu.make_async_copy(orecv, orecv, orecv_sem).wait()

    tri = orecv[...].astype(F32)
    mean = jnp.sum(tri, axis=0, keepdims=True) * (1.0 / 128)
    centered = tri - mean
    spread = jnp.sum(centered * centered, axis=0, keepdims=True) * (1.0 / 128)
    flat[...] = (centered * lax.rsqrt(spread + EPS)).reshape(1024, 128)
    out_gain = out_gain_ref[...]
    for s in range(8):
        normed = (flat[pl.ds(s, 128, stride=8), :].T * out_gain).astype(BF16)
        proj = jnp.dot(normed, out_w_ref[...], preferred_element_type=F32)
        rows_out[pl.ds(s, 64, stride=16), :] = proj[:64]
        rows_out[pl.ds(8 + s, 64, stride=16), :] = proj[64:]
    out_ref[...] = (gate[...] * rows_out[...]).astype(BF16).reshape(64, 16, 128)
    pltpu.make_async_copy(osend.at[pl.ds(0, CHIPS - 1)], osend.at[pl.ds(0, CHIPS - 1)], osend_sem).wait()


def body(pair, pair_mask, norm_gain, left_weight, right_weight, gate_weight, out_gain, out_weight):
    vmem = pl.BlockSpec(memory_space=pltpu.VMEM)
    return pl.pallas_call(
        kernel,
        out_shape=jax.ShapeDtypeStruct((64, 16, 128), BF16),
        in_specs=[vmem] * 8,
        out_specs=vmem,
        scratch_shapes=[
            pltpu.VMEM((1024, 128), F32),
            pltpu.VMEM((2, 1024, 128), F32),
            pltpu.VMEM((2048, 128), F32),
            pltpu.VMEM((128, 16, 128), BF16),
            pltpu.VMEM((128, 16, 128), BF16),
            pltpu.VMEM((2, 256, 512), F32),
            pltpu.VMEM((256, 512), F32),
            pltpu.VMEM((128, 8, 128), BF16),
            pltpu.VMEM((128, 8, 128), BF16),
            pltpu.VMEM((1024, 128), F32),
            pltpu.VMEM((1024, 128), F32),
        ] + [pltpu.SemaphoreType.DMA(())] * 6,
        compiler_params=pltpu.CompilerParams(
            collective_id=0, has_side_effects=True, vmem_limit_bytes=40 * 1024 * 1024,
        ),
        name="triangle",
    )(
        pair, pair_mask, norm_gain.reshape(1, 128), left_weight, right_weight, gate_weight,
        out_gain.reshape(1, 128), out_weight,
    )


def solution(mesh):
    in_specs = (P("row", "col", None), P("row", "col"), P(), P(), P(), P(), P(), P())
    out_specs = P("row", "col", None)
    return jax.shard_map(body, mesh=mesh, in_specs=in_specs, out_specs=out_specs, check_vma=False)
```

```python
import jax
import jax.numpy as jnp
from jax import lax
from jax.experimental import pallas as pl
from jax.experimental.pallas import tpu as pltpu
from jax.sharding import PartitionSpec as P

F32 = jnp.float32
BF16 = jnp.bfloat16
EPS = 1e-05
CHIPS = 128


def hops(offset):
    dz, dy, dx = offset
    return min(dz, 8 - dz) + min(dy, 4 - dy) + min(dx, 4 - dx)


OFFSETS = sorted(
    ((dz, dy, dx) for dx in range(4) for dy in range(4) for dz in range(8) if dz or dy or dx),
    key=lambda offset: -hops(offset),
)
CHUNKS = (2, 0, 1, 3)


def rem(a, b):
    return lax.rem(a, jnp.int32(b))


def div(a, b):
    return lax.div(a, jnp.int32(b))


def kernel(
    pair_hbm, mask_hbm, norm_gain_hbm, left_w_hbm, right_w_hbm, gate_w_hbm, out_gain_hbm, out_w_hbm,
    out_ref,
    pair_ref, mask_ref, norm_gain_ref, left_w_ref, right_w_ref, gate_w_ref, out_gain_ref, out_w_ref, load_sem,
    gate, edges, packed, send, recv, left, right, part, other, osend, orecv, flat, rows_out,
    send_sem, recv_sem, osend_sem, orecv_sem, xsend_sem, xrecv_sem,
):
    row = lax.axis_index("row")
    col = lax.axis_index("col")
    core = rem(col, 2)
    x = rem(row, 4)
    y = rem(div(col, 2), 4)
    z = div(row, 4) * 4 + div(col, 8)
    me = row * 16 + div(col, 2)

    z_at = [rem(z + d, 8) for d in range(8)]
    y_at = [rem(y + d, 4) for d in range(4)]
    x_at = [rem(x + d, 4) for d in range(4)]

    def peer(offset):
        dz, dy, dx = offset
        prow = div(z_at[dz], 4) * 4 + x_at[dx]
        pchip = rem(z_at[dz], 4) * 4 + y_at[dy]
        return prow * 16 + pchip, (prow, pchip * 2 + core)

    loads = [
        pltpu.make_async_copy(source, target, load_sem.at[at])
        for at, (source, target) in enumerate((
            (pair_hbm, pair_ref), (norm_gain_hbm, norm_gain_ref), (left_w_hbm, left_w_ref),
            (right_w_hbm, right_w_ref), (gate_w_hbm, gate_w_ref), (mask_hbm, mask_ref),
            (out_gain_hbm, out_gain_ref), (out_w_hbm, out_w_ref),
        ))
    ]
    for load in loads:
        load.start()

    partner = {"col": col + 1 - 2 * core}

    barrier = pltpu.get_barrier_semaphore()

    for offset in OFFSETS:
        pl.semaphore_signal(barrier, inc=1, device_id=peer(offset)[1], device_id_type=pl.DeviceIdType.MESH)
    pl.semaphore_signal(barrier, inc=1, device_id=partner, device_id_type=pl.DeviceIdType.MESH)

    for load in loads:
        load.wait()
    gain = norm_gain_ref[...]
    for block in range(4):
        values = pair_ref[pl.ds(block * 16, 16)].reshape(256, 128)
        mean = jnp.mean(values, axis=-1, keepdims=True)
        centered = values - mean
        spread = jnp.mean(centered * centered, axis=-1, keepdims=True)
        normed = (centered * lax.rsqrt(spread + EPS) * gain).astype(BF16)
        here = pl.ds(block * 256, 256)
        for side, weight in ((0, left_w_ref), (1, right_w_ref)):
            proj = jnp.dot(normed, weight[...], preferred_element_type=F32)
            edges[side, here, :] = jax.nn.sigmoid(proj[:, :128]) * proj[:, 128:]
        gate[here, :] = jax.nn.sigmoid(jnp.dot(normed, gate_w_ref[...], preferred_element_type=F32))

    odd = rem(row, 2)
    for k in range(16):
        first = edges[odd, pl.ds(k, 64, stride=16), :]
        second = edges[1 - odd, pl.ds(k, 64, stride=16), :]
        packed[pl.ds(k, 128, stride=16), :] = jnp.concatenate([first, second], axis=0).T
    mask = mask_ref[...].astype(F32)
    mask = jnp.concatenate([mask, mask], axis=1)
    send[...] = (packed[...].reshape(128, 16, 128) * mask[None]).astype(BF16)

    pl.semaphore_wait(barrier, CHIPS)

    own = pltpu.make_async_copy(send.at[me], recv.at[me], recv_sem)
    own.start()

    for offset in OFFSETS:
        there, device = peer(offset)
        pltpu.make_async_remote_copy(
            src_ref=send.at[there], dst_ref=recv.at[me], send_sem=send_sem, recv_sem=recv_sem,
            device_id=device, device_id_type=pl.DeviceIdType.MESH,
        ).start()
    pltpu.make_async_copy(recv, recv, recv_sem).wait()

    low = lax.broadcasted_iota(jnp.int32, (256, 128), 1) < 64
    for pair_at in range(4):
        even = recv[pl.ds(pair_at * 32, 16)].reshape(256, 128)
        uneven = recv[pl.ds(pair_at * 32 + 16, 16)].reshape(256, 128)
        here = pl.ds(pair_at * 256, 256)
        left[:, pair_at * 128:(pair_at + 1) * 128] = jnp.where(low, even, uneven)
        right[here, :] = jnp.where(low, uneven, even)

    swaps = []
    for at, dz in enumerate(CHUNKS):
        zone = rem(z_at[dz], 4)
        products = lax.dot_general(
            right[pl.ds(pl.multiple_of(zone * 256, 256), 256), :], left[...], (((0,), (0,)), ((), ())),
            preferred_element_type=F32,
        )
        for half in range(2):
            for q in range(4):
                source = half * 64 + q * 16
                part[at, q % 2, pl.ds((1 - half) * 32 + q // 2 * 16, 16), :] = products[source:source + 16]
        swap = pltpu.make_async_remote_copy(
            src_ref=part.at[at, 1 - core], dst_ref=other.at[at], send_sem=xsend_sem.at[at], recv_sem=xrecv_sem.at[at],
            device_id=partner, device_id_type=pl.DeviceIdType.MESH,
        )
        swap.start()
        swaps.append(swap)

    low8 = lax.broadcasted_iota(jnp.int32, (32, 128), 1) < 64
    own_back = pltpu.make_async_copy(osend.at[me], orecv.at[me], orecv_sem)
    for at, dz in enumerate(CHUNKS):
        swaps[at].wait_recv()
        zone = rem(z_at[dz], 4)
        for pair_at in range(4):
            lanes = pl.ds(pair_at * 128, 128)
            total = (part[at, core, :, lanes] + other[at, :, lanes]).reshape(4, 2, 8, 128)
            top = total[:, 0].reshape(32, 128)
            bottom = total[:, 1].reshape(32, 128)
            even = jnp.where(low8, top, pltpu.roll(bottom, 64, 1))
            uneven = jnp.where(low8, pltpu.roll(top, 64, 1), bottom)
            osend[pl.ds(pair_at * 32 + zone * 4, 4)] = even.reshape(4, 8, 128).astype(BF16)
            osend[pl.ds(pair_at * 32 + 16 + zone * 4, 4)] = uneven.reshape(4, 8, 128).astype(BF16)
        if dz == 0:
            own_back.start()
        for offset in OFFSETS:
            if offset[0] % 4 == dz:
                there, device = peer(offset)
                pltpu.make_async_remote_copy(
                    src_ref=osend.at[there], dst_ref=orecv.at[me], send_sem=osend_sem, recv_sem=orecv_sem,
                    device_id=device, device_id_type=pl.DeviceIdType.MESH,
                ).start()
    for swap in swaps:
        swap.wait_send()
    pltpu.make_async_copy(send.at[pl.ds(0, CHIPS - 1)], send.at[pl.ds(0, CHIPS - 1)], send_sem).wait()
    pltpu.make_async_copy(orecv, orecv, orecv_sem).wait()

    tri = orecv[...].astype(F32)
    mean = jnp.sum(tri, axis=0, keepdims=True) * (1.0 / 128)
    centered = tri - mean
    spread = jnp.sum(centered * centered, axis=0, keepdims=True) * (1.0 / 128)
    flat[...] = (centered * lax.rsqrt(spread + EPS)).reshape(1024, 128)
    out_gain = out_gain_ref[...]
    for s in range(8):
        normed = (flat[pl.ds(s, 128, stride=8), :].T * out_gain).astype(BF16)
        proj = jnp.dot(normed, out_w_ref[...], preferred_element_type=F32)
        rows_out[pl.ds(s, 64, stride=16), :] = proj[:64]
        rows_out[pl.ds(8 + s, 64, stride=16), :] = proj[64:]
    out_ref[...] = (gate[...] * rows_out[...]).astype(BF16).reshape(64, 16, 128)
    pltpu.make_async_copy(osend.at[pl.ds(0, CHIPS - 1)], osend.at[pl.ds(0, CHIPS - 1)], osend_sem).wait()


def body(pair, pair_mask, norm_gain, left_weight, right_weight, gate_weight, out_gain, out_weight):
    vmem = pl.BlockSpec(memory_space=pltpu.VMEM)
    return pl.pallas_call(
        kernel,
        out_shape=jax.ShapeDtypeStruct((64, 16, 128), BF16),
        in_specs=[pl.BlockSpec(memory_space=pltpu.HBM)] * 8,
        out_specs=vmem,
        scratch_shapes=[
            pltpu.VMEM((64, 16, 128), F32),
            pltpu.VMEM((16, 64), jnp.int32),
            pltpu.VMEM((1, 128), F32),
            pltpu.VMEM((128, 256), BF16),
            pltpu.VMEM((128, 256), BF16),
            pltpu.VMEM((128, 128), BF16),
            pltpu.VMEM((1, 128), F32),
            pltpu.VMEM((128, 128), BF16),
            pltpu.SemaphoreType.DMA((8,)),
            pltpu.VMEM((1024, 128), F32),
            pltpu.VMEM((2, 1024, 128), F32),
            pltpu.VMEM((2048, 128), F32),
            pltpu.VMEM((128, 16, 128), BF16),
            pltpu.VMEM((128, 16, 128), BF16),
            pltpu.VMEM((256, 512), BF16),
            pltpu.VMEM((1024, 128), BF16),
            pltpu.VMEM((4, 2, 64, 512), F32),
            pltpu.VMEM((4, 64, 512), F32),
            pltpu.VMEM((128, 8, 128), BF16),
            pltpu.VMEM((128, 8, 128), BF16),
            pltpu.VMEM((1024, 128), F32),
            pltpu.VMEM((1024, 128), F32),
        ] + [pltpu.SemaphoreType.DMA(())] * 4 + [pltpu.SemaphoreType.DMA((4,))] * 2,
        compiler_params=pltpu.CompilerParams(
            collective_id=0, has_side_effects=True, vmem_limit_bytes=56 * 1024 * 1024,
        ),
        name="triangle",
    )(
        pair, pair_mask.T, norm_gain.reshape(1, 128), left_weight, right_weight, gate_weight,
        out_gain.reshape(1, 128), out_weight,
    )


def solution(mesh):
    in_specs = (P("row", "col", None), P("row", "col"), P(), P(), P(), P(), P(), P())
    out_specs = P("row", "col", None)
    return jax.shard_map(body, mesh=mesh, in_specs=in_specs, out_specs=out_specs, check_vma=False)
```

```python
import jax
import jax.numpy as jnp
from jax import lax
from jax.experimental import pallas as pl
from jax.experimental.pallas import tpu as pltpu
from jax.sharding import PartitionSpec as P

F32 = jnp.float32
BF16 = jnp.bfloat16
EPS = 1e-05
CHIPS = 128


def hops(offset):
    dz, dy, dx = offset
    return min(dz, 8 - dz) + min(dy, 4 - dy) + min(dx, 4 - dx)


OFFSETS = sorted(
    ((dz, dy, dx) for dx in range(4) for dy in range(4) for dz in range(8) if dz or dy or dx),
    key=lambda offset: -hops(offset),
)
GREETED = sorted(
    ((dz, dy, dx, dc) for dc in range(2) for dx in range(2) for dy in range(4) for dz in range(8)),
    key=lambda offset: -hops((offset[0], offset[1], 2 * offset[2])),
)
BITS = [(zh, xs, yu, zt, dc) for zh in (1, 0) for xs in (1, 0) for yu in (1, 0) for zt in (1, 0) for dc in (0, 1)]
MESH = pl.DeviceIdType.MESH


def rem(a, b):
    return lax.rem(a, jnp.int32(b))


def div(a, b):
    return lax.div(a, jnp.int32(b))


def kernel(
    pair_hbm, mask_hbm, norm_gain_hbm, left_w_hbm, right_w_hbm, gate_w_hbm, out_gain_hbm, out_w_hbm,
    out_ref,
    pair_ref, mask_ref, norm_gain_ref, left_w_ref, right_w_ref, gate_w_ref, out_gain_ref, out_w_ref, load_sem,
    gate, edges, packed, send, recv, left, right, osend, orecv, flat, rows_out,
    send_sem, recv_sem, osend_sem, orecv_sem, xsend_sem, xrecv_sem,
):
    row = lax.axis_index("row")
    col = lax.axis_index("col")
    core = rem(col, 2)
    x = rem(row, 4)
    y = rem(div(col, 2), 4)
    z = div(row, 4) * 4 + div(col, 8)
    me = row * 16 + div(col, 2)

    z_at = [rem(z + d, 8) for d in range(8)]
    y_at = [rem(y + d, 4) for d in range(4)]
    x_at = [rem(x + d, 4) for d in range(4)]

    def peer(offset):
        dz, dy, dx = offset
        prow = div(z_at[dz], 4) * 4 + x_at[dx]
        pchip = rem(z_at[dz], 4) * 4 + y_at[dy]
        return prow * 16 + pchip, (prow, pchip * 2 + side)

    side = rem(x, 2)
    home = rem(x + core, 2)
    slot = (div(z, 4) * 2 + div(x, 2)) * 32 + col
    x_half = [rem(div(x, 2) + d, 2) for d in range(2)]
    core_at = [rem(core + d, 2) for d in range(2)]

    loads = [
        pltpu.make_async_copy(source, target, load_sem.at[at])
        for at, (source, target) in enumerate((
            (pair_hbm, pair_ref), (norm_gain_hbm, norm_gain_ref), (left_w_hbm, left_w_ref),
            (right_w_hbm, right_w_ref), (gate_w_hbm, gate_w_ref), (mask_hbm, mask_ref),
            (out_gain_hbm, out_gain_ref), (out_w_hbm, out_w_ref),
        ))
    ]
    for load in loads:
        load.start()

    partner = {"col": col + 1 - 2 * core}

    barrier = pltpu.get_barrier_semaphore()

    def greet(offset):
        dz, dy, dx, dc = offset
        device = (div(z_at[dz], 4) * 4 + core + 2 * x_half[dx], rem(z_at[dz], 4) * 8 + y_at[dy] * 2 + core_at[dc])
        pl.semaphore_signal(barrier, inc=1, device_id=device, device_id_type=MESH)

    for offset in GREETED:
        if offset[:3] != (0, 0, 0):
            greet(offset)
    pl.semaphore_signal(barrier, inc=1, device_id=partner, device_id_type=MESH)

    @pl.when(home != 0)
    def _():
        greet((0, 0, 0, 0))
        greet((0, 0, 0, 1))

    for load in loads:
        load.wait()
    gain = norm_gain_ref[...]
    for block in range(4):
        values = pair_ref[pl.ds(block * 16, 16)].reshape(256, 128)
        mean = jnp.mean(values, axis=-1, keepdims=True)
        centered = values - mean
        spread = jnp.mean(centered * centered, axis=-1, keepdims=True)
        normed = (centered * lax.rsqrt(spread + EPS) * gain).astype(BF16)
        here = pl.ds(block * 256, 256)
        for which, weight in ((0, left_w_ref), (1, right_w_ref)):
            proj = jnp.dot(normed, weight[...], preferred_element_type=F32)
            edges[which, here, :] = jax.nn.sigmoid(proj[:, :128]) * proj[:, 128:]
        gate[here, :] = jax.nn.sigmoid(jnp.dot(normed, gate_w_ref[...], preferred_element_type=F32))

    odd = div(x, 2)
    for k in range(16):
        first = edges[odd, pl.ds(k, 64, stride=16), :]
        second = edges[1 - odd, pl.ds(k, 64, stride=16), :]
        packed[pl.ds(k, 128, stride=16), :] = jnp.concatenate([first, second], axis=0).T
    mask = mask_ref[...].astype(F32)
    mask = jnp.concatenate([mask, mask], axis=1)
    send[...] = (packed[...].reshape(128, 16, 128) * mask[None]).astype(BF16)

    pl.semaphore_wait(barrier, CHIPS)

    @pl.when(home == 0)
    def _():
        pltpu.make_async_copy(send.at[me], recv.at[slot], recv_sem).start()

    @pl.when(home != 0)
    def _():
        pltpu.make_async_remote_copy(
            src_ref=send.at[me], dst_ref=recv.at[slot], send_sem=send_sem, recv_sem=recv_sem,
            device_id=partner, device_id_type=MESH,
        ).start()

    for offset in OFFSETS:
        there, device = peer(offset)
        pltpu.make_async_remote_copy(
            src_ref=send.at[there], dst_ref=recv.at[slot], send_sem=send_sem, recv_sem=recv_sem,
            device_id=device, device_id_type=MESH,
        ).start()
    pltpu.make_async_copy(recv, recv, recv_sem).wait()

    low = lax.broadcasted_iota(jnp.int32, (512, 128), 1) < 64
    swaps = []
    for zh in range(2):
        first = recv[pl.ds(zh * 64, 32)].reshape(512, 128)
        second = recv[pl.ds(zh * 64 + 32, 32)].reshape(512, 128)
        left[:, zh * 128:(zh + 1) * 128] = jnp.where(low, first, second)
        right[0, zh] = jnp.where(low, second, first)
    for zh in range(2):
        swap = pltpu.make_async_remote_copy(
            src_ref=right.at[0, zh], dst_ref=right.at[1, zh], send_sem=xsend_sem.at[zh], recv_sem=xrecv_sem.at[zh],
            device_id=partner, device_id_type=MESH,
        )
        swap.start()
        swaps.append(swap)

    low8 = lax.broadcasted_iota(jnp.int32, (64, 128), 1) < 64
    for whose in range(2):
        if whose == 1:
            for swap in swaps:
                swap.wait_recv()
        x_low = core if whose == 0 else 1 - core
        for dp in (1, 0):
            zone = rem(div(rem(z, 4), 2) + dp, 2)
            products = lax.dot_general(
                right[whose, zone], left[...], (((0,), (0,)), ((), ())), preferred_element_type=F32
            )
            for zh in range(2):
                block = products[:, zh * 128:(zh + 1) * 128].reshape(8, 2, 8, 128)
                top = block[:, 0].reshape(64, 128)
                bottom = block[:, 1].reshape(64, 128)
                even = jnp.where(low8, top, pltpu.roll(bottom, 64, 1)).reshape(8, 8, 128).astype(BF16)
                uneven = jnp.where(low8, pltpu.roll(top, 64, 1), bottom).reshape(8, 8, 128).astype(BF16)
                for xs, values in ((0, even), (1, uneven)):
                    for half in range(2):
                        at = (zh * 2 + xs) * 32 + zone * 16 + (1 - half) * 8 + x_low * 4
                        osend[pl.ds(at, 4)] = values[half * 4:half * 4 + 4]

            def give_back(bits):
                zh, xs, yu, zt, dc = bits
                pz = rem(div(z, 4) + zh, 2)
                prow = pz * 4 + core + 2 * x_half[xs]
                pcol = (zone * 2 + rem(z + zt, 2)) * 8 + (2 * x_low + rem(y + yu, 2)) * 2 + core_at[dc]
                return (pz * 2 + x_half[xs]) * 32 + pcol, (prow, pcol)

            def send_back(bits):
                there, device = give_back(bits)
                pltpu.make_async_remote_copy(
                    src_ref=osend.at[there], dst_ref=orecv.at[me], send_sem=osend_sem, recv_sem=orecv_sem,
                    device_id=device, device_id_type=MESH,
                ).start()

            for bits in BITS:
                if dp == 0 and bits == (0, 0, 0, 0, 0):
                    mine = home + lax.abs(div(y, 2) - x_low) == 0

                    @pl.when(mine)
                    def _():
                        pltpu.make_async_copy(osend.at[slot], orecv.at[me], orecv_sem).start()

                    @pl.when(jnp.logical_not(mine))
                    def _():
                        send_back(bits)
                else:
                    send_back(bits)
    for swap in swaps:
        swap.wait_send()
    pltpu.make_async_copy(send.at[pl.ds(0, CHIPS - 1)], send.at[pl.ds(0, CHIPS - 1)], send_sem).wait()

    @pl.when(home != 0)
    def _():
        pltpu.make_async_copy(send.at[0], send.at[0], send_sem).wait()
    pltpu.make_async_copy(orecv, orecv, orecv_sem).wait()

    tri = orecv[...].astype(F32)
    mean = jnp.sum(tri, axis=0, keepdims=True) * (1.0 / 128)
    centered = tri - mean
    spread = jnp.sum(centered * centered, axis=0, keepdims=True) * (1.0 / 128)
    flat[...] = (centered * lax.rsqrt(spread + EPS)).reshape(1024, 128)
    out_gain = out_gain_ref[...]
    for s in range(8):
        normed = (flat[pl.ds(s, 128, stride=8), :].T * out_gain).astype(BF16)
        proj = jnp.dot(normed, out_w_ref[...], preferred_element_type=F32)
        rows_out[pl.ds(s, 64, stride=16), :] = proj[:64]
        rows_out[pl.ds(8 + s, 64, stride=16), :] = proj[64:]
    out_ref[...] = (gate[...] * rows_out[...]).astype(BF16).reshape(64, 16, 128)
    pltpu.make_async_copy(osend.at[pl.ds(0, CHIPS - 1)], osend.at[pl.ds(0, CHIPS - 1)], osend_sem).wait()

    @pl.when(home != 0)
    def _():
        pltpu.make_async_copy(osend.at[0], osend.at[0], osend_sem).wait()


def body(pair, pair_mask, norm_gain, left_weight, right_weight, gate_weight, out_gain, out_weight):
    vmem = pl.BlockSpec(memory_space=pltpu.VMEM)
    return pl.pallas_call(
        kernel,
        out_shape=pltpu.VMEM((64, 16, 128), BF16),
        in_specs=[pl.BlockSpec(memory_space=pltpu.HBM)] * 8,
        out_specs=vmem,
        scratch_shapes=[
            pltpu.VMEM((64, 16, 128), F32),
            pltpu.VMEM((16, 64), jnp.int32),
            pltpu.VMEM((1, 128), F32),
            pltpu.VMEM((128, 256), BF16),
            pltpu.VMEM((128, 256), BF16),
            pltpu.VMEM((128, 128), BF16),
            pltpu.VMEM((1, 128), F32),
            pltpu.VMEM((128, 128), BF16),
            pltpu.SemaphoreType.DMA((8,)),
            pltpu.VMEM((1024, 128), F32),
            pltpu.VMEM((2, 1024, 128), F32),
            pltpu.VMEM((2048, 128), F32),
            pltpu.VMEM((128, 16, 128), BF16),
            pltpu.VMEM((128, 16, 128), BF16),
            pltpu.VMEM((512, 256), BF16),
            pltpu.VMEM((2, 2, 512, 128), BF16),
            pltpu.VMEM((128, 8, 128), BF16),
            pltpu.VMEM((128, 8, 128), BF16),
            pltpu.VMEM((1024, 128), F32),
            pltpu.VMEM((1024, 128), F32),
        ] + [pltpu.SemaphoreType.DMA(())] * 4 + [pltpu.SemaphoreType.DMA((2,))] * 2,
        compiler_params=pltpu.CompilerParams(
            collective_id=0, has_side_effects=True, vmem_limit_bytes=40 * 1024 * 1024,
        ),
        name="triangle",
    )(
        *(pltpu.with_memory_space_constraint(a, pltpu.HBM) for a in (pair, pair_mask.T, norm_gain.reshape(1, 128), left_weight, right_weight, gate_weight,
        out_gain.reshape(1, 128), out_weight))
    )


def solution(mesh):
    in_specs = (P("row", "col", None), P("row", "col"), P(), P(), P(), P(), P(), P())
    out_specs = P("row", "col", None)
    return jax.shard_map(body, mesh=mesh, in_specs=in_specs, out_specs=out_specs, check_vma=False)
```

```python
import jax
import jax.numpy as jnp
from jax import lax
from jax.experimental import pallas as pl
from jax.experimental.pallas import tpu as pltpu
from jax.sharding import PartitionSpec as P

F32 = jnp.float32
BF16 = jnp.bfloat16
EPS = 1e-05
CHIPS = 128


def hops(offset):
    dz, dy, dx = offset
    return min(dz, 8 - dz) + min(dy, 4 - dy) + min(dx, 4 - dx)


OFFSETS = sorted(
    ((dz, dy, dx) for dx in range(4) for dy in range(4) for dz in range(8) if dz or dy or dx),
    key=lambda offset: -hops(offset),
)
MESH = pl.DeviceIdType.MESH


def rem(a, b):
    return lax.rem(a, jnp.int32(b))


def div(a, b):
    return lax.div(a, jnp.int32(b))


def kernel(
    pair_hbm, mask_hbm, norm_gain_hbm, left_w_hbm, right_w_hbm, gate_w_hbm, out_gain_hbm, out_w_hbm,
    out_ref,
    pair_ref, mask_ref, norm_gain_ref, left_w_ref, right_w_ref, gate_w_ref, out_gain_ref, out_w_ref, load_sem,
    gate, edges, packed, send_left, send_right, mixed, recv, recv_right, left, right, osend, orecv, flat, rows_out,
    send_sem, recv_sem, mix_send_sem, mix_recv_sem, swap_send_sem, swap_recv_sem, osend_sem, orecv_sem,
):
    row = lax.axis_index("row")
    col = lax.axis_index("col")
    core = rem(col, 2)
    x = rem(row, 4)
    y = rem(div(col, 2), 4)
    z = div(row, 4) * 4 + div(col, 8)
    me = row * 16 + div(col, 2)

    z_at = [rem(z + d, 8) for d in range(8)]
    y_at = [rem(y + d, 4) for d in range(4)]
    x_at = [rem(x + d, 4) for d in range(4)]

    def peer(offset):
        dz, dy, dx = offset
        prow = div(z_at[dz], 4) * 4 + x_at[dx]
        pchip = rem(z_at[dz], 4) * 4 + y_at[dy]
        return prow * 16 + pchip, (prow, pchip * 2 + core)

    loads = [
        pltpu.make_async_copy(source, target, load_sem.at[at])
        for at, (source, target) in enumerate((
            (pair_hbm, pair_ref), (norm_gain_hbm, norm_gain_ref), (left_w_hbm, left_w_ref),
            (right_w_hbm, right_w_ref), (gate_w_hbm, gate_w_ref), (mask_hbm, mask_ref),
            (out_gain_hbm, out_gain_ref), (out_w_hbm, out_w_ref),
        ))
    ]
    for load in loads:
        load.start()

    partner = {"col": col + 1 - 2 * core}

    barrier = pltpu.get_barrier_semaphore()

    for offset in OFFSETS:
        pl.semaphore_signal(barrier, inc=1, device_id=peer(offset)[1], device_id_type=MESH)
    pl.semaphore_signal(barrier, inc=1, device_id=partner, device_id_type=MESH)

    for load in loads:
        load.wait()
    gain = norm_gain_ref[...]
    for block in range(4):
        values = pair_ref[pl.ds(block * 16, 16)].reshape(256, 128)
        mean = jnp.mean(values, axis=-1, keepdims=True)
        centered = values - mean
        spread = jnp.mean(centered * centered, axis=-1, keepdims=True)
        normed = (centered * lax.rsqrt(spread + EPS) * gain).astype(BF16)
        here = pl.ds(block * 256, 256)
        for which, weight in ((0, left_w_ref), (1, right_w_ref)):
            proj = jnp.dot(normed, weight[...], preferred_element_type=F32)
            edges[which, here, :] = jax.nn.sigmoid(proj[:, :128]) * proj[:, 128:]
        gate[here, :] = jax.nn.sigmoid(jnp.dot(normed, gate_w_ref[...], preferred_element_type=F32))

    mask = mask_ref[...].astype(F32)
    left_mask = jnp.concatenate([mask[:8], mask[8:]], axis=1)
    right_lanes = [(high, q) for parity in range(2) for high in range(2) for q in (parity, parity + 2)]
    right_mask = jnp.concatenate([mask[high * 8:high * 8 + 8, q * 16:q * 16 + 16] for high, q in right_lanes], axis=1)
    for k in range(8):
        rows = [edges[0, pl.ds(high * 8 + k, 64, stride=16), :] for high in range(2)]
        packed[0, pl.ds(k, 128, stride=8), :] = jnp.concatenate(rows, axis=0).T
    send_left[...] = (packed[0].reshape(128, 8, 128) * left_mask[None]).astype(BF16)
    for k in range(8):
        rows = [edges[1, pl.ds(q * 256 + high * 8 + k, 16, stride=16), :] for high, q in right_lanes]
        packed[1, pl.ds(k, 128, stride=8), :] = jnp.concatenate(rows, axis=0).T
    mixed[0] = (packed[1].reshape(128, 8, 128) * right_mask[None]).astype(BF16)

    pl.semaphore_wait(barrier, CHIPS)

    def scatter(source, target, sem):
        pltpu.make_async_copy(source.at[me], target.at[me], sem).start()
        for offset in OFFSETS:
            there, device = peer(offset)
            pltpu.make_async_remote_copy(
                src_ref=source.at[there], dst_ref=target.at[me], send_sem=send_sem, recv_sem=sem,
                device_id=device, device_id_type=MESH,
            ).start()

    mix = pltpu.make_async_remote_copy(
        src_ref=mixed.at[0], dst_ref=mixed.at[1], send_sem=mix_send_sem, recv_sem=mix_recv_sem,
        device_id=partner, device_id_type=MESH,
    )
    mix.start()
    scatter(send_left, recv.at[0], recv_sem.at[0])
    mix.wait_recv()
    mine = lax.broadcasted_iota(jnp.int32, (1024, 128), 1) // 64 == core
    theirs = pltpu.roll(mixed[1].astype(F32).reshape(1024, 128), 64, 1)
    send_right[...] = jnp.where(mine, mixed[0].astype(F32).reshape(1024, 128), theirs).reshape(128, 8, 128).astype(BF16)
    scatter(send_right, recv_right, recv_sem.at[1])

    pltpu.make_async_copy(recv.at[0], recv.at[0], recv_sem.at[0]).wait()
    swap = pltpu.make_async_remote_copy(
        src_ref=recv.at[0], dst_ref=recv.at[1], send_sem=swap_send_sem, recv_sem=swap_recv_sem,
        device_id=partner, device_id_type=MESH,
    )
    swap.start()
    low = lax.broadcasted_iota(jnp.int32, (128, 128), 1) < 64
    for whose in range(2):
        if whose == 1:
            swap.wait_recv()
        tokens = pl.multiple_of((core if whose == 0 else 1 - core) * 256, 256)
        for pair_at in range(4):
            first = recv[whose, pl.ds(pair_at * 32, 16)].astype(F32).reshape(128, 128)
            second = recv[whose, pl.ds(pair_at * 32 + 16, 16)].astype(F32).reshape(128, 128)
            lanes = pl.ds(pair_at * 128, 128)
            left[pl.ds(tokens, 128), lanes] = jnp.where(low, first, pltpu.roll(second, 64, 1)).astype(BF16)
            left[pl.ds(tokens + 128, 128), lanes] = jnp.where(low, pltpu.roll(first, 64, 1), second).astype(BF16)

    pltpu.make_async_copy(recv_right, recv_right, recv_sem.at[1]).wait()
    for r in range(8):
        turned = recv_right[pl.ds(r * 16, 16)].astype(F32).reshape(128, 128).astype(BF16).T
        for group in range(4):
            right[pl.ds(r * 32, 32), pl.ds(group * 128, 128)] = turned[group * 32:group * 32 + 32]

    low8 = lax.broadcasted_iota(jnp.int32, (128, 128), 1) < 64
    for quarter in range(4):
        products = jnp.dot(
            right[...], left[:, quarter * 128:(quarter + 1) * 128], preferred_element_type=F32
        ).reshape(16, 2, 8, 128)
        top = products[:, 0].reshape(128, 128)
        bottom = products[:, 1].reshape(128, 128)
        even = jnp.where(low8, top, pltpu.roll(bottom, 64, 1))
        uneven = jnp.where(low8, pltpu.roll(top, 64, 1), bottom)
        osend[pl.ds(quarter * 32, 16)] = even.reshape(16, 8, 128).astype(BF16)
        osend[pl.ds(quarter * 32 + 16, 16)] = uneven.reshape(16, 8, 128).astype(BF16)

    pltpu.make_async_copy(osend.at[me], orecv.at[me], orecv_sem).start()
    for offset in OFFSETS:
        there, device = peer(offset)
        pltpu.make_async_remote_copy(
            src_ref=osend.at[there], dst_ref=orecv.at[me], send_sem=osend_sem, recv_sem=orecv_sem,
            device_id=device, device_id_type=MESH,
        ).start()

    mix.wait_send()
    swap.wait_send()
    for source in (send_left, send_right):
        pltpu.make_async_copy(source.at[pl.ds(0, CHIPS - 1)], source.at[pl.ds(0, CHIPS - 1)], send_sem).wait()
    pltpu.make_async_copy(orecv, orecv, orecv_sem).wait()

    tri = orecv[...].astype(F32)
    mean = jnp.sum(tri, axis=0, keepdims=True) * (1.0 / 128)
    centered = tri - mean
    spread = jnp.sum(centered * centered, axis=0, keepdims=True) * (1.0 / 128)
    flat[...] = (centered * lax.rsqrt(spread + EPS)).reshape(1024, 128)
    out_gain = out_gain_ref[...]
    for s in range(8):
        normed = (flat[pl.ds(s, 128, stride=8), :].T * out_gain).astype(BF16)
        proj = jnp.dot(normed, out_w_ref[...], preferred_element_type=F32)
        rows_out[pl.ds(s, 64, stride=16), :] = proj[:64]
        rows_out[pl.ds(8 + s, 64, stride=16), :] = proj[64:]
    out_ref[...] = (gate[...] * rows_out[...]).astype(BF16).reshape(64, 16, 128)
    pltpu.make_async_copy(osend.at[pl.ds(0, CHIPS - 1)], osend.at[pl.ds(0, CHIPS - 1)], osend_sem).wait()


def body(pair, pair_mask, norm_gain, left_weight, right_weight, gate_weight, out_gain, out_weight):
    vmem = pl.BlockSpec(memory_space=pltpu.VMEM)
    return pl.pallas_call(
        kernel,
        out_shape=pltpu.VMEM((64, 16, 128), BF16),
        in_specs=[pl.BlockSpec(memory_space=pltpu.HBM)] * 8,
        out_specs=vmem,
        scratch_shapes=[
            pltpu.VMEM((64, 16, 128), F32),
            pltpu.VMEM((16, 64), jnp.int32),
            pltpu.VMEM((1, 128), F32),
            pltpu.VMEM((128, 256), BF16),
            pltpu.VMEM((128, 256), BF16),
            pltpu.VMEM((128, 128), BF16),
            pltpu.VMEM((1, 128), F32),
            pltpu.VMEM((128, 128), BF16),
            pltpu.SemaphoreType.DMA((8,)),
            pltpu.VMEM((1024, 128), F32),
            pltpu.VMEM((2, 1024, 128), F32),
            pltpu.VMEM((2, 1024, 128), F32),
            pltpu.VMEM((128, 8, 128), BF16),
            pltpu.VMEM((128, 8, 128), BF16),
            pltpu.VMEM((2, 128, 8, 128), BF16),
            pltpu.VMEM((2, 128, 8, 128), BF16),
            pltpu.VMEM((128, 8, 128), BF16),
            pltpu.VMEM((512, 512), BF16),
            pltpu.VMEM((256, 512), BF16),
            pltpu.VMEM((128, 8, 128), BF16),
            pltpu.VMEM((128, 8, 128), BF16),
            pltpu.VMEM((1024, 128), F32),
            pltpu.VMEM((1024, 128), F32),
        ] + [pltpu.SemaphoreType.DMA(())] + [pltpu.SemaphoreType.DMA((2,))] + [pltpu.SemaphoreType.DMA(())] * 6,
        compiler_params=pltpu.CompilerParams(
            collective_id=0, has_side_effects=True, vmem_limit_bytes=40 * 1024 * 1024,
        ),
        name="triangle",
    )(
        *(pltpu.with_memory_space_constraint(a, pltpu.HBM) for a in (pair, pair_mask.T, norm_gain.reshape(1, 128), left_weight, right_weight, gate_weight,
        out_gain.reshape(1, 128), out_weight))
    )


def solution(mesh):
    in_specs = (P("row", "col", None), P("row", "col"), P(), P(), P(), P(), P(), P())
    out_specs = P("row", "col", None)
    return jax.shard_map(body, mesh=mesh, in_specs=in_specs, out_specs=out_specs, check_vma=False)
```

```python
import jax
import jax.numpy as jnp
from jax import lax
from jax.experimental import pallas as pl
from jax.experimental.pallas import tpu as pltpu
from jax.sharding import PartitionSpec as P

F32 = jnp.float32
BF16 = jnp.bfloat16
EPS = 1e-05
CHIPS = 128


def hops(offset):
    dz, dy, dx = offset
    return min(dz, 8 - dz) + min(dy, 4 - dy) + min(dx, 4 - dx)


def offsets(weight):
    every = [(dz, dy, dx) for dx in range(4) for dy in range(4) for dz in range(8) if dz or dy or dx]
    along_z = lambda offset: min(offset[0], 8 - offset[0])
    return sorted(every, key=lambda offset: (-hops(offset) + (1 - weight) * along_z(offset), along_z(offset)))


LEFT_ORDER, RIGHT_ORDER, BACK_ORDER = offsets(0.5), offsets(1), offsets(0.5)
MESH = pl.DeviceIdType.MESH


def rem(a, b):
    return lax.rem(a, jnp.int32(b))


def div(a, b):
    return lax.div(a, jnp.int32(b))


def kernel(
    pair_hbm, mask_hbm, norm_gain_hbm, left_w_hbm, right_w_hbm, gate_w_hbm, out_gain_hbm, out_w_hbm,
    out_ref,
    pair_ref, mask_ref, norm_gain_ref, left_w_ref, right_w_ref, gate_w_ref, out_gain_ref, out_w_ref, load_sem,
    gate, edges, packed, send_left, send_right, mixed, recv, recv_right, left, right, osend, orecv, flat, rows_out,
    send_sem, recv_sem, mix_send_sem, mix_recv_sem, swap_send_sem, swap_recv_sem, osend_sem, orecv_sem,
):
    row = lax.axis_index("row")
    col = lax.axis_index("col")
    core = rem(col, 2)
    x = rem(row, 4)
    y = rem(div(col, 2), 4)
    z = div(row, 4) * 4 + div(col, 8)
    me = row * 16 + div(col, 2)

    z_at = [rem(z + d, 8) for d in range(8)]
    y_at = [rem(y + d, 4) for d in range(4)]
    x_at = [rem(x + d, 4) for d in range(4)]

    def peer(offset):
        dz, dy, dx = offset
        prow = div(z_at[dz], 4) * 4 + x_at[dx]
        pchip = rem(z_at[dz], 4) * 4 + y_at[dy]
        return prow * 16 + pchip, (prow, pchip * 2 + core)

    loads = [
        pltpu.make_async_copy(source, target, load_sem.at[at])
        for at, (source, target) in enumerate((
            (pair_hbm, pair_ref), (norm_gain_hbm, norm_gain_ref), (left_w_hbm, left_w_ref),
            (right_w_hbm, right_w_ref), (gate_w_hbm, gate_w_ref), (mask_hbm, mask_ref),
            (out_gain_hbm, out_gain_ref), (out_w_hbm, out_w_ref),
        ))
    ]
    for load in loads:
        load.start()

    partner = {"col": col + 1 - 2 * core}

    barrier = pltpu.get_barrier_semaphore()

    for offset in BACK_ORDER:
        pl.semaphore_signal(barrier, inc=1, device_id=peer(offset)[1], device_id_type=MESH)
    pl.semaphore_signal(barrier, inc=1, device_id=partner, device_id_type=MESH)

    for load in loads:
        load.wait()
    gain = norm_gain_ref[...]
    for block in range(4):
        values = pair_ref[pl.ds(block * 16, 16)].reshape(256, 128)
        mean = jnp.mean(values, axis=-1, keepdims=True)
        centered = values - mean
        spread = jnp.mean(centered * centered, axis=-1, keepdims=True)
        normed = (centered * lax.rsqrt(spread + EPS) * gain).astype(BF16)
        here = pl.ds(block * 256, 256)
        for which, weight in ((0, left_w_ref), (1, right_w_ref)):
            proj = jnp.dot(normed, weight[...], preferred_element_type=F32)
            edges[which, here, :] = jax.nn.sigmoid(proj[:, :128]) * proj[:, 128:]
        gate[here, :] = jax.nn.sigmoid(jnp.dot(normed, gate_w_ref[...], preferred_element_type=F32))

    mask = mask_ref[...].astype(F32)
    left_mask = jnp.concatenate([mask[:8], mask[8:]], axis=1)
    right_lanes = [(high, q) for parity in range(2) for high in range(2) for q in (parity, parity + 2)]
    right_mask = jnp.concatenate([mask[high * 8:high * 8 + 8, q * 16:q * 16 + 16] for high, q in right_lanes], axis=1)
    for k in range(8):
        rows = [edges[0, pl.ds(high * 8 + k, 64, stride=16), :] for high in range(2)]
        packed[0, pl.ds(k, 128, stride=8), :] = jnp.concatenate(rows, axis=0).T
    send_left[...] = (packed[0].reshape(128, 8, 128) * left_mask[None]).astype(BF16)
    for k in range(8):
        rows = [edges[1, pl.ds(q * 256 + high * 8 + k, 16, stride=16), :] for high, q in right_lanes]
        packed[1, pl.ds(k, 128, stride=8), :] = jnp.concatenate(rows, axis=0).T
    mixed[0] = (packed[1].reshape(128, 8, 128) * right_mask[None]).astype(BF16)

    pl.semaphore_wait(barrier, CHIPS)

    def scatter(source, target, sem, order):
        pltpu.make_async_copy(source.at[me], target.at[me], sem).start()
        for offset in order:
            there, device = peer(offset)
            pltpu.make_async_remote_copy(
                src_ref=source.at[there], dst_ref=target.at[me], send_sem=send_sem, recv_sem=sem,
                device_id=device, device_id_type=MESH,
            ).start()

    mix = pltpu.make_async_remote_copy(
        src_ref=mixed.at[0], dst_ref=mixed.at[1], send_sem=mix_send_sem, recv_sem=mix_recv_sem,
        device_id=partner, device_id_type=MESH,
    )
    mix.start()
    scatter(send_left, recv.at[0], recv_sem.at[0], LEFT_ORDER)
    mix.wait_recv()
    mine = lax.broadcasted_iota(jnp.int32, (1024, 128), 1) // 64 == core
    theirs = pltpu.roll(mixed[1].astype(F32).reshape(1024, 128), 64, 1)
    send_right[...] = jnp.where(mine, mixed[0].astype(F32).reshape(1024, 128), theirs).reshape(128, 8, 128).astype(BF16)
    scatter(send_right, recv_right, recv_sem.at[1], RIGHT_ORDER)

    pltpu.make_async_copy(recv.at[0], recv.at[0], recv_sem.at[0]).wait()
    swap = pltpu.make_async_remote_copy(
        src_ref=recv.at[0], dst_ref=recv.at[1], send_sem=swap_send_sem, recv_sem=swap_recv_sem,
        device_id=partner, device_id_type=MESH,
    )
    swap.start()
    low = lax.broadcasted_iota(jnp.int32, (128, 128), 1) < 64
    for whose in range(2):
        if whose == 1:
            swap.wait_recv()
        tokens = pl.multiple_of((core if whose == 0 else 1 - core) * 256, 256)
        for pair_at in range(4):
            first = recv[whose, pl.ds(pair_at * 32, 16)].astype(F32).reshape(128, 128)
            second = recv[whose, pl.ds(pair_at * 32 + 16, 16)].astype(F32).reshape(128, 128)
            lanes = pl.ds(pair_at * 128, 128)
            left[pl.ds(tokens, 128), lanes] = jnp.where(low, first, pltpu.roll(second, 64, 1)).astype(BF16)
            left[pl.ds(tokens + 128, 128), lanes] = jnp.where(low, pltpu.roll(first, 64, 1), second).astype(BF16)

    pltpu.make_async_copy(recv_right, recv_right, recv_sem.at[1]).wait()
    for r in range(8):
        turned = recv_right[pl.ds(r * 16, 16)].astype(F32).reshape(128, 128).astype(BF16).T
        for group in range(4):
            right[pl.ds(r * 32, 32), pl.ds(group * 128, 128)] = turned[group * 32:group * 32 + 32]

    low8 = lax.broadcasted_iota(jnp.int32, (128, 128), 1) < 64
    for quarter in range(4):
        products = jnp.dot(
            right[...], left[:, quarter * 128:(quarter + 1) * 128], preferred_element_type=F32
        ).reshape(16, 2, 8, 128)
        top = products[:, 0].reshape(128, 128)
        bottom = products[:, 1].reshape(128, 128)
        even = jnp.where(low8, top, pltpu.roll(bottom, 64, 1))
        uneven = jnp.where(low8, pltpu.roll(top, 64, 1), bottom)
        osend[pl.ds(quarter * 32, 16)] = even.reshape(16, 8, 128).astype(BF16)
        osend[pl.ds(quarter * 32 + 16, 16)] = uneven.reshape(16, 8, 128).astype(BF16)

    pltpu.make_async_copy(osend.at[me], orecv.at[me], orecv_sem).start()
    for offset in BACK_ORDER:
        there, device = peer(offset)
        pltpu.make_async_remote_copy(
            src_ref=osend.at[there], dst_ref=orecv.at[me], send_sem=osend_sem, recv_sem=orecv_sem,
            device_id=device, device_id_type=MESH,
        ).start()

    mix.wait_send()
    swap.wait_send()
    for source in (send_left, send_right):
        pltpu.make_async_copy(source.at[pl.ds(0, CHIPS - 1)], source.at[pl.ds(0, CHIPS - 1)], send_sem).wait()
    pltpu.make_async_copy(orecv, orecv, orecv_sem).wait()

    tri = orecv[...].astype(F32)
    mean = jnp.sum(tri, axis=0, keepdims=True) * (1.0 / 128)
    centered = tri - mean
    spread = jnp.sum(centered * centered, axis=0, keepdims=True) * (1.0 / 128)
    flat[...] = (centered * lax.rsqrt(spread + EPS)).reshape(1024, 128)
    out_gain = out_gain_ref[...]
    for s in range(8):
        normed = (flat[pl.ds(s, 128, stride=8), :].T * out_gain).astype(BF16)
        proj = jnp.dot(normed, out_w_ref[...], preferred_element_type=F32)
        rows_out[pl.ds(s, 64, stride=16), :] = proj[:64]
        rows_out[pl.ds(8 + s, 64, stride=16), :] = proj[64:]
    out_ref[...] = (gate[...] * rows_out[...]).astype(BF16).reshape(64, 16, 128)
    pltpu.make_async_copy(osend.at[pl.ds(0, CHIPS - 1)], osend.at[pl.ds(0, CHIPS - 1)], osend_sem).wait()


def body(pair, pair_mask, norm_gain, left_weight, right_weight, gate_weight, out_gain, out_weight):
    vmem = pl.BlockSpec(memory_space=pltpu.VMEM)
    return pl.pallas_call(
        kernel,
        out_shape=pltpu.VMEM((64, 16, 128), BF16),
        in_specs=[pl.BlockSpec(memory_space=pltpu.HBM)] * 8,
        out_specs=vmem,
        scratch_shapes=[
            pltpu.VMEM((64, 16, 128), F32),
            pltpu.VMEM((16, 64), jnp.int32),
            pltpu.VMEM((1, 128), F32),
            pltpu.VMEM((128, 256), BF16),
            pltpu.VMEM((128, 256), BF16),
            pltpu.VMEM((128, 128), BF16),
            pltpu.VMEM((1, 128), F32),
            pltpu.VMEM((128, 128), BF16),
            pltpu.SemaphoreType.DMA((8,)),
            pltpu.VMEM((1024, 128), F32),
            pltpu.VMEM((2, 1024, 128), F32),
            pltpu.VMEM((2, 1024, 128), F32),
            pltpu.VMEM((128, 8, 128), BF16),
            pltpu.VMEM((128, 8, 128), BF16),
            pltpu.VMEM((2, 128, 8, 128), BF16),
            pltpu.VMEM((2, 128, 8, 128), BF16),
            pltpu.VMEM((128, 8, 128), BF16),
            pltpu.VMEM((512, 512), BF16),
            pltpu.VMEM((256, 512), BF16),
            pltpu.VMEM((128, 8, 128), BF16),
            pltpu.VMEM((128, 8, 128), BF16),
            pltpu.VMEM((1024, 128), F32),
            pltpu.VMEM((1024, 128), F32),
        ] + [pltpu.SemaphoreType.DMA(())] + [pltpu.SemaphoreType.DMA((2,))] + [pltpu.SemaphoreType.DMA(())] * 6,
        compiler_params=pltpu.CompilerParams(
            collective_id=0, has_side_effects=True, vmem_limit_bytes=40 * 1024 * 1024,
        ),
        name="triangle",
    )(
        *(pltpu.with_memory_space_constraint(a, pltpu.HBM) for a in (pair, pair_mask.T, norm_gain.reshape(1, 128), left_weight, right_weight, gate_weight,
        out_gain.reshape(1, 128), out_weight))
    )


def solution(mesh):
    in_specs = (P("row", "col", None), P("row", "col"), P(), P(), P(), P(), P(), P())
    out_specs = P("row", "col", None)
    return jax.shard_map(body, mesh=mesh, in_specs=in_specs, out_specs=out_specs, check_vma=False)
```

```python
import jax
import jax.numpy as jnp
from jax import lax
from jax.experimental import pallas as pl
from jax.experimental.pallas import tpu as pltpu
from jax.sharding import PartitionSpec as P

F32 = jnp.float32
BF16 = jnp.bfloat16
EPS = 1e-05
CHIPS = 128


def hops(offset):
    dz, dy, dx = offset
    return min(dz, 8 - dz) + min(dy, 4 - dy) + min(dx, 4 - dx)


def offsets(weight):
    every = [(dz, dy, dx) for dx in range(4) for dy in range(4) for dz in range(8) if dz or dy or dx]
    along_z = lambda offset: min(offset[0], 8 - offset[0])
    return sorted(every, key=lambda offset: (-hops(offset) + (1 - weight) * along_z(offset), along_z(offset)))


LEFT_ORDER, RIGHT_ORDER, BACK_ORDER = offsets(0.5), offsets(1), offsets(0.5)
MESH = pl.DeviceIdType.MESH


def rem(a, b):
    return lax.rem(a, jnp.int32(b))


def div(a, b):
    return lax.div(a, jnp.int32(b))


def kernel(
    pair_hbm, mask_hbm, norm_gain_hbm, left_w_hbm, right_w_hbm, gate_w_hbm, out_gain_hbm, out_w_hbm,
    out_ref,
    pair_ref, mask_ref, norm_gain_ref, left_w_ref, right_w_ref, gate_w_ref, out_gain_ref, out_w_ref, load_sem,
    gate, edges, packed, send_left, send_right, mixed, recv, recv_right, left, right, osend, orecv, flat, rows_out,
    send_sem, recv_sem, mix_send_sem, mix_recv_sem, swap_send_sem, swap_recv_sem, osend_sem, orecv_sem,
):
    row = lax.axis_index("row")
    col = lax.axis_index("col")
    core = rem(col, 2)
    x = rem(row, 4)
    y = rem(div(col, 2), 4)
    z = div(row, 4) * 4 + div(col, 8)
    me = row * 16 + div(col, 2)

    z_at = [rem(z + d, 8) for d in range(8)]
    y_at = [rem(y + d, 4) for d in range(4)]
    x_at = [rem(x + d, 4) for d in range(4)]

    def peer(offset):
        dz, dy, dx = offset
        prow = div(z_at[dz], 4) * 4 + x_at[dx]
        pchip = rem(z_at[dz], 4) * 4 + y_at[dy]
        return prow * 16 + pchip, (prow, pchip * 2 + core)

    loads = [
        pltpu.make_async_copy(source, target, load_sem.at[at])
        for at, (source, target) in enumerate((
            (pair_hbm, pair_ref), (norm_gain_hbm, norm_gain_ref), (left_w_hbm, left_w_ref),
            (right_w_hbm, right_w_ref), (gate_w_hbm, gate_w_ref), (mask_hbm, mask_ref),
            (out_gain_hbm, out_gain_ref), (out_w_hbm, out_w_ref),
        ))
    ]
    for load in loads:
        load.start()

    partner = {"col": col + 1 - 2 * core}

    barrier = pltpu.get_barrier_semaphore()

    for offset in RIGHT_ORDER:
        pl.semaphore_signal(barrier, inc=1, device_id=peer(offset)[1], device_id_type=MESH)
    pl.semaphore_signal(barrier, inc=1, device_id=partner, device_id_type=MESH)

    for load in loads:
        load.wait()
    gain = norm_gain_ref[...]
    for block in range(4):
        values = pair_ref[pl.ds(block * 16, 16)].reshape(256, 128)
        mean = jnp.mean(values, axis=-1, keepdims=True)
        centered = values - mean
        spread = jnp.mean(centered * centered, axis=-1, keepdims=True)
        normed = (centered * lax.rsqrt(spread + EPS) * gain).astype(BF16)
        here = pl.ds(block * 256, 256)
        for which, weight in ((0, left_w_ref), (1, right_w_ref)):
            proj = jnp.dot(normed, weight[...], preferred_element_type=F32)
            edges[which, here, :] = jax.nn.sigmoid(proj[:, :128]) * proj[:, 128:]
        gate[here, :] = jax.nn.sigmoid(jnp.dot(normed, gate_w_ref[...], preferred_element_type=F32))

    mask = mask_ref[...].astype(F32)
    left_mask = jnp.concatenate([mask[:8], mask[8:]], axis=1)
    right_lanes = [(high, q) for parity in range(2) for high in range(2) for q in (parity, parity + 2)]
    right_mask = jnp.concatenate([mask[high * 8:high * 8 + 8, q * 16:q * 16 + 16] for high, q in right_lanes], axis=1)
    for k in range(8):
        rows = [edges[0, pl.ds(high * 8 + k, 64, stride=16), :] for high in range(2)]
        packed[0, pl.ds(k, 128, stride=8), :] = jnp.concatenate(rows, axis=0).T
    send_left[...] = (packed[0].reshape(128, 8, 128) * left_mask[None]).astype(BF16)
    for k in range(8):
        rows = [edges[1, pl.ds(q * 256 + high * 8 + k, 16, stride=16), :] for high, q in right_lanes]
        packed[1, pl.ds(k, 128, stride=8), :] = jnp.concatenate(rows, axis=0).T
    mixed[0] = (packed[1].reshape(128, 8, 128) * right_mask[None]).astype(BF16)

    pl.semaphore_wait(barrier, CHIPS)

    def scatter(source, target, sem, order):
        pltpu.make_async_copy(source.at[me], target.at[me], sem).start()
        for offset in order:
            there, device = peer(offset)
            pltpu.make_async_remote_copy(
                src_ref=source.at[there], dst_ref=target.at[me], send_sem=send_sem, recv_sem=sem,
                device_id=device, device_id_type=MESH,
            ).start()

    mix = pltpu.make_async_remote_copy(
        src_ref=mixed.at[0], dst_ref=mixed.at[1], send_sem=mix_send_sem, recv_sem=mix_recv_sem,
        device_id=partner, device_id_type=MESH,
    )
    mix.start()
    scatter(send_left, recv.at[0], recv_sem.at[0], LEFT_ORDER)
    mix.wait_recv()
    mine = lax.broadcasted_iota(jnp.int32, (1024, 128), 1) // 64 == core
    theirs = pltpu.roll(mixed[1].astype(F32).reshape(1024, 128), 64, 1)
    send_right[...] = jnp.where(mine, mixed[0].astype(F32).reshape(1024, 128), theirs).reshape(128, 8, 128).astype(BF16)
    scatter(send_right, recv_right, recv_sem.at[1], RIGHT_ORDER)

    pltpu.make_async_copy(recv.at[0], recv.at[0], recv_sem.at[0]).wait()
    swap = pltpu.make_async_remote_copy(
        src_ref=recv.at[0], dst_ref=recv.at[1], send_sem=swap_send_sem, recv_sem=swap_recv_sem,
        device_id=partner, device_id_type=MESH,
    )
    swap.start()
    low = lax.broadcasted_iota(jnp.int32, (128, 128), 1) < 64
    for whose in range(2):
        if whose == 1:
            swap.wait_recv()
        tokens = pl.multiple_of((core if whose == 0 else 1 - core) * 256, 256)
        for pair_at in range(4):
            first = recv[whose, pl.ds(pair_at * 32, 16)].astype(F32).reshape(128, 128)
            second = recv[whose, pl.ds(pair_at * 32 + 16, 16)].astype(F32).reshape(128, 128)
            lanes = pl.ds(pair_at * 128, 128)
            left[pl.ds(tokens, 128), lanes] = jnp.where(low, first, pltpu.roll(second, 64, 1)).astype(BF16)
            left[pl.ds(tokens + 128, 128), lanes] = jnp.where(low, pltpu.roll(first, 64, 1), second).astype(BF16)

    pltpu.make_async_copy(recv_right, recv_right, recv_sem.at[1]).wait()
    for r in range(8):
        turned = recv_right[pl.ds(r * 16, 16)].astype(F32).reshape(128, 128).astype(BF16).T
        for group in range(4):
            right[pl.ds(r * 32, 32), pl.ds(group * 128, 128)] = turned[group * 32:group * 32 + 32]

    low8 = lax.broadcasted_iota(jnp.int32, (128, 128), 1) < 64
    for half in range(2):
        products = jnp.dot(right[...], left[:, half * 256:(half + 1) * 256], preferred_element_type=F32)
        for pair_at in range(2):
            at = half * 64 + pair_at * 32
            blocks = products[:, pair_at * 128:(pair_at + 1) * 128].reshape(16, 2, 8, 128)
            top = blocks[:, 0].reshape(128, 128)
            bottom = blocks[:, 1].reshape(128, 128)
            even = jnp.where(low8, top, pltpu.roll(bottom, 64, 1))
            uneven = jnp.where(low8, pltpu.roll(top, 64, 1), bottom)
            osend[pl.ds(at, 16)] = even.reshape(16, 8, 128).astype(BF16)
            osend[pl.ds(at + 16, 16)] = uneven.reshape(16, 8, 128).astype(BF16)

    pltpu.make_async_copy(osend.at[me], orecv.at[me], orecv_sem).start()
    for offset in BACK_ORDER:
        there, device = peer(offset)
        pltpu.make_async_remote_copy(
            src_ref=osend.at[there], dst_ref=orecv.at[me], send_sem=osend_sem, recv_sem=orecv_sem,
            device_id=device, device_id_type=MESH,
        ).start()

    mix.wait_send()
    swap.wait_send()
    for source in (send_left, send_right):
        pltpu.make_async_copy(source.at[pl.ds(0, CHIPS - 1)], source.at[pl.ds(0, CHIPS - 1)], send_sem).wait()
    pltpu.make_async_copy(orecv, orecv, orecv_sem).wait()

    tri = orecv[...].astype(F32)
    mean = jnp.sum(tri, axis=0, keepdims=True) * (1.0 / 128)
    centered = tri - mean
    spread = jnp.sum(centered * centered, axis=0, keepdims=True) * (1.0 / 128)
    flat[...] = (centered * lax.rsqrt(spread + EPS)).reshape(1024, 128)
    out_gain = out_gain_ref[...]
    for s in range(8):
        normed = (flat[pl.ds(s, 128, stride=8), :].T * out_gain).astype(BF16)
        proj = jnp.dot(normed, out_w_ref[...], preferred_element_type=F32)
        rows_out[pl.ds(s, 64, stride=16), :] = proj[:64]
        rows_out[pl.ds(8 + s, 64, stride=16), :] = proj[64:]
    out_ref[...] = (gate[...] * rows_out[...]).astype(BF16).reshape(64, 16, 128)
    pltpu.make_async_copy(osend.at[pl.ds(0, CHIPS - 1)], osend.at[pl.ds(0, CHIPS - 1)], osend_sem).wait()


def body(pair, pair_mask, norm_gain, left_weight, right_weight, gate_weight, out_gain, out_weight):
    vmem = pl.BlockSpec(memory_space=pltpu.VMEM)
    return pl.pallas_call(
        kernel,
        out_shape=pltpu.VMEM((64, 16, 128), BF16),
        in_specs=[pl.BlockSpec(memory_space=pltpu.HBM)] * 8,
        out_specs=vmem,
        scratch_shapes=[
            pltpu.VMEM((64, 16, 128), F32),
            pltpu.VMEM((16, 64), jnp.int32),
            pltpu.VMEM((1, 128), F32),
            pltpu.VMEM((128, 256), BF16),
            pltpu.VMEM((128, 256), BF16),
            pltpu.VMEM((128, 128), BF16),
            pltpu.VMEM((1, 128), F32),
            pltpu.VMEM((128, 128), BF16),
            pltpu.SemaphoreType.DMA((8,)),
            pltpu.VMEM((1024, 128), F32),
            pltpu.VMEM((2, 1024, 128), F32),
            pltpu.VMEM((2, 1024, 128), F32),
            pltpu.VMEM((128, 8, 128), BF16),
            pltpu.VMEM((128, 8, 128), BF16),
            pltpu.VMEM((2, 128, 8, 128), BF16),
            pltpu.VMEM((2, 128, 8, 128), BF16),
            pltpu.VMEM((128, 8, 128), BF16),
            pltpu.VMEM((512, 512), BF16),
            pltpu.VMEM((256, 512), BF16),
            pltpu.VMEM((128, 8, 128), BF16),
            pltpu.VMEM((128, 8, 128), BF16),
            pltpu.VMEM((1024, 128), F32),
            pltpu.VMEM((1024, 128), F32),
        ] + [pltpu.SemaphoreType.DMA(())] + [pltpu.SemaphoreType.DMA((2,))] + [pltpu.SemaphoreType.DMA(())] * 6,
        compiler_params=pltpu.CompilerParams(
            collective_id=0, has_side_effects=True, vmem_limit_bytes=40 * 1024 * 1024,
        ),
        name="triangle",
    )(
        *(pltpu.with_memory_space_constraint(a, pltpu.HBM) for a in (pair, pair_mask.T, norm_gain.reshape(1, 128), left_weight, right_weight, gate_weight,
        out_gain.reshape(1, 128), out_weight))
    )


def solution(mesh):
    in_specs = (P("row", "col", None), P("row", "col"), P(), P(), P(), P(), P(), P())
    out_specs = P("row", "col", None)
    return jax.shard_map(body, mesh=mesh, in_specs=in_specs, out_specs=out_specs, check_vma=False)
```

```python
import jax
import jax.numpy as jnp
from jax import lax
from jax.experimental import pallas as pl
from jax.experimental.pallas import tpu as pltpu
from jax.sharding import PartitionSpec as P

F32 = jnp.float32
BF16 = jnp.bfloat16
EPS = 1e-05
CHIPS = 128


def hops(offset):
    dz, dy, dx = offset
    return min(dz, 8 - dz) + min(dy, 4 - dy) + min(dx, 4 - dx)


def offsets(weight):
    every = [(dz, dy, dx) for dx in range(4) for dy in range(4) for dz in range(8) if dz or dy or dx]
    along_z = lambda offset: min(offset[0], 8 - offset[0])
    return sorted(every, key=lambda offset: (-hops(offset) + (1 - weight) * along_z(offset), along_z(offset)))


LEFT_ORDER, RIGHT_ORDER, BACK_ORDER = offsets(0.5), offsets(1), offsets(0.5)
MESH = pl.DeviceIdType.MESH


def rem(a, b):
    return lax.rem(a, jnp.int32(b))


def div(a, b):
    return lax.div(a, jnp.int32(b))


def kernel(
    pair_hbm, mask_hbm, norm_gain_hbm, left_w_hbm, right_w_hbm, gate_w_hbm, out_gain_hbm, out_w_hbm,
    out_ref,
    pair_ref, mask_ref, norm_gain_ref, left_w_ref, right_w_ref, gate_w_ref, out_gain_ref, out_w_ref, load_sem,
    gate, edges, packed, send_left, send_right, mixed, recv, recv_right, left, right, osend, orecv, flat, rows_out,
    send_sem, recv_sem, mix_send_sem, mix_recv_sem, swap_send_sem, swap_recv_sem, osend_sem, orecv_sem,
):
    row = lax.axis_index("row")
    col = lax.axis_index("col")
    core = rem(col, 2)
    x = rem(row, 4)
    y = rem(div(col, 2), 4)
    z = div(row, 4) * 4 + div(col, 8)
    me = row * 16 + div(col, 2)

    z_at = [rem(z + d, 8) for d in range(8)]
    y_at = [rem(y + d, 4) for d in range(4)]
    x_at = [rem(x + d, 4) for d in range(4)]

    def peer(offset):
        dz, dy, dx = offset
        prow = div(z_at[dz], 4) * 4 + x_at[dx]
        pchip = rem(z_at[dz], 4) * 4 + y_at[dy]
        return prow * 16 + pchip, (prow, pchip * 2 + core)

    loads = [
        pltpu.make_async_copy(source, target, load_sem.at[at])
        for at, (source, target) in enumerate((
            (pair_hbm, pair_ref), (norm_gain_hbm, norm_gain_ref), (left_w_hbm, left_w_ref),
            (right_w_hbm, right_w_ref), (gate_w_hbm, gate_w_ref), (mask_hbm, mask_ref),
            (out_gain_hbm, out_gain_ref), (out_w_hbm, out_w_ref),
        ))
    ]
    for load in loads:
        load.start()

    partner = {"col": col + 1 - 2 * core}

    barrier = pltpu.get_barrier_semaphore()

    for offset in RIGHT_ORDER:
        pl.semaphore_signal(barrier, inc=1, device_id=peer(offset)[1], device_id_type=MESH)
    pl.semaphore_signal(barrier, inc=1, device_id=partner, device_id_type=MESH)

    for load in loads:
        load.wait()
    gain = norm_gain_ref[...]
    for block in range(4):
        values = pair_ref[pl.ds(block * 16, 16)].reshape(256, 128)
        mean = jnp.mean(values, axis=-1, keepdims=True)
        centered = values - mean
        spread = jnp.mean(centered * centered, axis=-1, keepdims=True)
        normed = (centered * lax.rsqrt(spread + EPS) * gain).astype(BF16)
        here = pl.ds(block * 256, 256)
        for which, weight in ((0, left_w_ref), (1, right_w_ref)):
            proj = jnp.dot(normed, weight[...], preferred_element_type=F32)
            edges[which, here, :] = jax.nn.sigmoid(proj[:, :128]) * proj[:, 128:]
        gate[here, :] = jax.nn.sigmoid(jnp.dot(normed, gate_w_ref[...], preferred_element_type=F32))

    mask = mask_ref[...].astype(F32)
    left_mask = jnp.concatenate([mask[:8], mask[8:]], axis=1)
    right_lanes = [(high, q) for parity in range(2) for high in range(2) for q in (parity, parity + 2)]
    right_mask = jnp.concatenate([mask[high * 8:high * 8 + 8, q * 16:q * 16 + 16] for high, q in right_lanes], axis=1)
    for k in range(8):
        rows = [edges[0, pl.ds(high * 8 + k, 64, stride=16), :] for high in range(2)]
        packed[0, pl.ds(k, 128, stride=8), :] = jnp.concatenate(rows, axis=0).T
    send_left[...] = (packed[0].reshape(128, 8, 128) * left_mask[None]).astype(BF16)
    for k in range(8):
        rows = [edges[1, pl.ds(q * 256 + high * 8 + k, 16, stride=16), :] for high, q in right_lanes]
        packed[1, pl.ds(k, 128, stride=8), :] = jnp.concatenate(rows, axis=0).T
    mixed[0] = (packed[1].reshape(128, 8, 128) * right_mask[None]).astype(BF16)

    pl.semaphore_wait(barrier, CHIPS)

    def scatter(source, target, sem, order):
        pltpu.make_async_copy(source.at[me], target.at[me], sem).start()
        for offset in order:
            there, device = peer(offset)
            pltpu.make_async_remote_copy(
                src_ref=source.at[there], dst_ref=target.at[me], send_sem=send_sem, recv_sem=sem,
                device_id=device, device_id_type=MESH,
            ).start()

    mix = pltpu.make_async_remote_copy(
        src_ref=mixed.at[0], dst_ref=mixed.at[1], send_sem=mix_send_sem, recv_sem=mix_recv_sem,
        device_id=partner, device_id_type=MESH,
    )
    mix.start()
    scatter(send_left, recv.at[0], recv_sem.at[0], LEFT_ORDER)
    mix.wait_recv()
    mine = lax.broadcasted_iota(jnp.int32, (1024, 128), 1) // 64 == core
    theirs = pltpu.roll(mixed[1].astype(F32).reshape(1024, 128), 64, 1)
    send_right[...] = jnp.where(mine, mixed[0].astype(F32).reshape(1024, 128), theirs).reshape(128, 8, 128).astype(BF16)
    scatter(send_right, recv_right, recv_sem.at[1], RIGHT_ORDER)

    pltpu.make_async_copy(recv.at[0], recv.at[0], recv_sem.at[0]).wait()
    swap = pltpu.make_async_remote_copy(
        src_ref=recv.at[0], dst_ref=recv.at[1], send_sem=swap_send_sem, recv_sem=swap_recv_sem,
        device_id=partner, device_id_type=MESH,
    )
    swap.start()
    low = lax.broadcasted_iota(jnp.int32, (128, 128), 1) < 64
    for whose in range(2):
        if whose == 1:
            swap.wait_recv()
        tokens = pl.multiple_of((core if whose == 0 else 1 - core) * 256, 256)
        for pair_at in range(4):
            first = recv[whose, pl.ds(pair_at * 32, 16)].astype(F32).reshape(128, 128)
            second = recv[whose, pl.ds(pair_at * 32 + 16, 16)].astype(F32).reshape(128, 128)
            lanes = pl.ds(pair_at * 128, 128)
            left[pl.ds(tokens, 128), lanes] = jnp.where(low, first, pltpu.roll(second, 64, 1)).astype(BF16)
            left[pl.ds(tokens + 128, 128), lanes] = jnp.where(low, pltpu.roll(first, 64, 1), second).astype(BF16)

    pltpu.make_async_copy(recv_right, recv_right, recv_sem.at[1]).wait()
    for r in range(8):
        turned = recv_right[pl.ds(r * 16, 16)].astype(F32).reshape(128, 128).astype(BF16).T
        for group in range(4):
            right[pl.ds(r * 32, 32), pl.ds(group * 128, 128)] = turned[group * 32:group * 32 + 32]

    low8 = lax.broadcasted_iota(jnp.int32, (128, 128), 1) < 64
    for half in range(2):
        products = jnp.dot(right[...], left[:, half * 256:(half + 1) * 256], preferred_element_type=F32)
        for pair_at in range(2):
            at = half * 64 + pair_at * 32
            blocks = products[:, pair_at * 128:(pair_at + 1) * 128].reshape(16, 2, 8, 128)
            top = blocks[:, 0].reshape(128, 128)
            bottom = blocks[:, 1].reshape(128, 128)
            even = jnp.where(low8, top, pltpu.roll(bottom, 64, 1))
            uneven = jnp.where(low8, pltpu.roll(top, 64, 1), bottom)
            osend[pl.ds(at, 16)] = even.reshape(16, 8, 128).astype(BF16)
            osend[pl.ds(at + 16, 16)] = uneven.reshape(16, 8, 128).astype(BF16)

    pltpu.make_async_copy(osend.at[me], orecv.at[me], orecv_sem).start()
    for offset in BACK_ORDER:
        there, device = peer(offset)
        pltpu.make_async_remote_copy(
            src_ref=osend.at[there], dst_ref=orecv.at[me], send_sem=osend_sem, recv_sem=orecv_sem,
            device_id=device, device_id_type=MESH,
        ).start()

    mix.wait_send()
    swap.wait_send()
    for source in (send_left, send_right):
        pltpu.make_async_copy(source.at[pl.ds(0, CHIPS - 1)], source.at[pl.ds(0, CHIPS - 1)], send_sem).wait()
    pltpu.make_async_copy(orecv, orecv, orecv_sem).wait()

    tri = orecv[...].astype(F32)
    mean = jnp.sum(tri, axis=0, keepdims=True) * (1.0 / 128)
    centered = tri - mean
    spread = jnp.sum(centered * centered, axis=0, keepdims=True) * (1.0 / 128)
    flat[...] = (centered * lax.rsqrt(spread + EPS)).reshape(1024, 128)
    out_gain = out_gain_ref[...]
    normed = jnp.concatenate(
        [(flat[pl.ds(s, 128, stride=8), :].T * out_gain).astype(BF16) for s in range(8)], axis=0
    )
    proj = jnp.dot(normed, out_w_ref[...], preferred_element_type=F32)
    for s in range(8):
        rows_out[pl.ds(s, 64, stride=16), :] = proj[s * 128:s * 128 + 64]
        rows_out[pl.ds(8 + s, 64, stride=16), :] = proj[s * 128 + 64:s * 128 + 128]
    out_ref[...] = (gate[...] * rows_out[...]).astype(BF16).reshape(64, 16, 128)
    pltpu.make_async_copy(osend.at[pl.ds(0, CHIPS - 1)], osend.at[pl.ds(0, CHIPS - 1)], osend_sem).wait()


def body(pair, pair_mask, norm_gain, left_weight, right_weight, gate_weight, out_gain, out_weight):
    vmem = pl.BlockSpec(memory_space=pltpu.VMEM)
    return pl.pallas_call(
        kernel,
        out_shape=pltpu.VMEM((64, 16, 128), BF16),
        in_specs=[pl.BlockSpec(memory_space=pltpu.HBM)] * 8,
        out_specs=vmem,
        scratch_shapes=[
            pltpu.VMEM((64, 16, 128), F32),
            pltpu.VMEM((16, 64), jnp.int32),
            pltpu.VMEM((1, 128), F32),
            pltpu.VMEM((128, 256), BF16),
            pltpu.VMEM((128, 256), BF16),
            pltpu.VMEM((128, 128), BF16),
            pltpu.VMEM((1, 128), F32),
            pltpu.VMEM((128, 128), BF16),
            pltpu.SemaphoreType.DMA((8,)),
            pltpu.VMEM((1024, 128), F32),
            pltpu.VMEM((2, 1024, 128), F32),
            pltpu.VMEM((2, 1024, 128), F32),
            pltpu.VMEM((128, 8, 128), BF16),
            pltpu.VMEM((128, 8, 128), BF16),
            pltpu.VMEM((2, 128, 8, 128), BF16),
            pltpu.VMEM((2, 128, 8, 128), BF16),
            pltpu.VMEM((128, 8, 128), BF16),
            pltpu.VMEM((512, 512), BF16),
            pltpu.VMEM((256, 512), BF16),
            pltpu.VMEM((128, 8, 128), BF16),
            pltpu.VMEM((128, 8, 128), BF16),
            pltpu.VMEM((1024, 128), F32),
            pltpu.VMEM((1024, 128), F32),
        ] + [pltpu.SemaphoreType.DMA(())] + [pltpu.SemaphoreType.DMA((2,))] + [pltpu.SemaphoreType.DMA(())] * 6,
        compiler_params=pltpu.CompilerParams(
            collective_id=0, has_side_effects=True, vmem_limit_bytes=40 * 1024 * 1024,
        ),
        name="triangle",
    )(
        *(pltpu.with_memory_space_constraint(a, pltpu.HBM) for a in (pair, pair_mask.T, norm_gain.reshape(1, 128), left_weight, right_weight, gate_weight,
        out_gain.reshape(1, 128), out_weight))
    )


def solution(mesh):
    in_specs = (P("row", "col", None), P("row", "col"), P(), P(), P(), P(), P(), P())
    out_specs = P("row", "col", None)
    return jax.shard_map(body, mesh=mesh, in_specs=in_specs, out_specs=out_specs, check_vma=False)
```
